32 devices in a mesh: run: 2 (over y), area: 16 (over z, x, core).
Axes of the slice: x: 2, y: 2, z: 4, core: 2. Of those that a mesh axis runs over, the one named last changes fastest.
Arguments:
- pattern: int32 [2048, 128, 128], P('area'), may hold values from 0 to 1999
- target_area: int32 [2048, 1], replicated, may hold values from 0 to 15; in each aligned block of 128 rows (0 to 127, 128 to 255, ...) at most 16 rows name the same one
- source_block: int32 [2048], replicated, may hold values from 0 to 3
- target_block: int32 [2048], replicated, may hold values from 0 to 3
- neuron_lag: int32 [8192], replicated, may hold values from 0 to 15
- tau_mem: float32 [8192], P('area'), may hold values from 1 to 20
- v_init: float32 [16384], P(('run', 'area')), parts along dimension 0, may hold values from -4 to 4
- ext_count: int32 [10, 16384], P(None, ('run', 'area')), parts along dimension 1, may hold values from 0 to 3
Outputs:
- membrane: float32 [16384], P(('run', 'area')), parts along dimension 0
- activity: bfloat16 [10, 16384], P(None, ('run', 'area')), parts along dimension 1
- pending: float32 [15, 16384], P(None, ('run', 'area')), parts along dimension 1
The draws below stay inside these ranges and needn't reach their ends.
There are 2 independent parts, one for each index of `run`. The reference program is written for one: setup_inputs(seed, part) draws one part's arguments, and reference() takes and returns one part's arrays. A program takes and returns all parts, laid end to end along the dimension named above; an argument that names none is the same for every part. Nothing has to cross between parts.
Inputs may be any that keep to these rules, and one draw needn't show every extreme that they name: `target_area`: among the 128 rows of one builder no area is named more than 16 times, a bound that some block reaches.
All inputs are finite; a program needn't handle non-finite values.
Results may differ from the reference program's by a relative error of at most 0.0038.
Values may be sent and summed in bfloat16 or wider, within the bound.
A program may use at most 128 MiB of HBM per device.

```python
import math
import jax
import jax.numpy as jnp
import numpy as np
from jax import lax

BLK = 128
NB = 4
OUT_DEV = 128
STEPS = 10
DELAYS = 15
LAGS = 16
CAP = 16
NEURONS = 8192
EDGES = 2048
N_AREA = 16


def plant(array, key, low, high):
    shape = array.shape
    index_at = [jax.random.randint(jax.random.fold_in(key, axis), (), 0, shape[axis]) for axis in range(len(shape))]
    array = array.at[tuple(index_at)].set(low)
    longest = shape.index(max(shape))
    index_at[longest] = (index_at[longest] + 1) % shape[longest]
    return array.at[tuple(index_at)].set(high)


def levels(key, extent, shards, least, high):
    factor_of = 1.0
    for axis_at, blocks in shards:
        heights = jax.random.uniform(jax.random.fold_in(jax.random.fold_in(key, 6), axis_at), (blocks,), jnp.float32, least / len(shards), high / len(shards))
        factor_of = factor_of * jnp.repeat(jnp.exp(heights), extent[axis_at] // blocks).reshape((-1,) + (1,) * (len(extent) - 1 - axis_at))
    return factor_of


def shared_out(rng, own, number, rows, amount, top, most, skew):
    ranking = jax.random.permutation(rng, amount)
    heavy_load, ordinary = shares(amount, rows * top, most, skew, True), shares(amount, rows * top, most, skew, False)
    places = jnp.arange(amount)

    def named(lengths, offset_by):
        used = int((lengths > 0).sum())
        fixed = max(1, used // 4)
        passed = fixed + (places - fixed + offset_by * (used - fixed)) % max(1, amount - fixed)
        return jnp.zeros((amount,), jnp.int32).at[ranking[jnp.where(places < fixed, places, passed)]].set(jnp.asarray(lengths, jnp.int32))

    lengths = jnp.where(number % 4 == 0, named(heavy_load, number // 4), named(ordinary, number - number // 4 - 1))
    mixed = jax.random.permutation(jax.random.fold_in(own, 3), amount)
    giver, sink = mixed[0:amount // 2 * 2:2], mixed[1:amount // 2 * 2:2]
    slack = jnp.minimum(lengths[giver] - 1, most - lengths[sink]) // 2
    slack = jnp.where((giver == ranking[0]) | (sink == ranking[0]) | (lengths[sink] == 0), 0, jnp.maximum(slack, 0))
    passed = jax.random.randint(jax.random.fold_in(own, 4), (amount // 2,), 0, 1 << 20) % (slack + 1)
    lengths = lengths.at[giver].add(-passed).at[sink].add(passed)
    members = jnp.searchsorted(jnp.cumsum(lengths), jnp.arange(rows * top), side="right").astype(jnp.int32)
    listing = members.reshape(top, rows).T
    listing = listing[jax.random.permutation(jax.random.fold_in(own, 1), rows)]
    offset_by = jax.random.randint(jax.random.fold_in(own, 2), (rows, 1), 0, top)
    return jnp.take_along_axis(listing, (jnp.arange(top)[None, :] + offset_by) % top, axis=1)


def shares(number_of, total, most, lean, full):
    weights = [(1 << 20) // math.isqrt(standing ** lean) + 1 for standing in range(1, number_of + 1)]
    largest = most if full else min(most, max(-(-total // number_of), total * weights[0] // sum(weights)))
    least = 1 if total - largest >= number_of - 1 else 0
    holding, spare = [largest] + [least] * (number_of - 1), total - largest - least * (number_of - 1)
    while spare > 0:
        movable = [i for i in range(1, number_of) if holding[i] < largest] or [i for i in range(1, number_of) if holding[i] < most]
        pool, left = sum([weights[i] for i in movable]), spare
        for i in movable:
            extra = min(most - holding[i], max(1, left * weights[i] // pool), spare)
            holding[i] = holding[i] + extra
            spare = spare - extra
    return np.array(holding)


def normal_values(own_key, extent, width, reach, split=(), kind=jnp.bfloat16):
    result = jax.random.normal(own_key, extent, jnp.float32) * width
    if len(split) > 0:
        result = levels(own_key, extent, split, -0.22, 0.18) * result
    return jnp.clip(result, min=-reach, max=reach).astype(kind)


def setup_inputs(seed: int = 0, part: int = 0) -> dict:
    streams_of = jax.random.split(jax.random.key(seed), 9)
    own_keys = jax.random.split(jax.random.fold_in(streams_of[8], part), 9)
    pattern = plant(jax.random.randint(streams_of[0], (EDGES, BLK, BLK), 0, 2000), jax.random.fold_in(streams_of[0], 1), 0, 1999).astype(jnp.int32)
    target_area_keys = jax.random.split(jax.random.fold_in(streams_of[1], 1), EDGES // OUT_DEV)
    target_area_turns = jax.random.permutation(jax.random.fold_in(streams_of[1], 3), EDGES // OUT_DEV)
    target_area = jax.vmap(lambda own, number: shared_out(jax.random.fold_in(streams_of[1], 2), own, number, OUT_DEV, N_AREA, 1, CAP, 2))(target_area_keys, target_area_turns).reshape((EDGES, 1))
    source_block = plant(jax.random.randint(streams_of[2], (EDGES,), 0, NB), jax.random.fold_in(streams_of[2], 1), 0, NB - 1).astype(jnp.int32)
    target_block = plant(jax.random.randint(streams_of[3], (EDGES,), 0, NB), jax.random.fold_in(streams_of[3], 1), 0, NB - 1).astype(jnp.int32)
    neuron_lag = plant(jax.random.randint(streams_of[4], (NEURONS,), 0, LAGS), jax.random.fold_in(streams_of[4], 1), 0, LAGS - 1).astype(jnp.int32)
    tau_mem = jnp.clip(jnp.exp(math.log(20.0) - 2.9957323 * jax.random.uniform(streams_of[5], (NEURONS,), jnp.float32) ** levels(streams_of[5], (NEURONS,), ((0, 16),), -0.2, 0.2)), 1.0, 20.0)
    v_init = normal_values(own_keys[6], (NEURONS,), 0.7, 4.0, ((0, 16),), jnp.float32)
    ext_count = plant(jax.random.randint(own_keys[7], (STEPS, NEURONS), 0, 4), jax.random.fold_in(own_keys[7], 1), 0, 3).astype(jnp.int32)
    return {"pattern": pattern, "target_area": target_area, "source_block": source_block, "target_block": target_block, "neuron_lag": neuron_lag, "tau_mem": tau_mem, "v_init": v_init, "ext_count": ext_count}


step_ms = 0.1
ext_gain = 0.25
threshold = 1.0
slope = 4.0
reset_part = 0.5
inhib_gain = 3.0

def block_weights(pattern_rows, source_rows):
    factor = 8.0 / math.sqrt(BLK * OUT_DEV / NB)
    magnitude = jnp.maximum(pattern_rows.astype(jnp.float32) - 999.0, 0.0) / 1000.0
    signs = jnp.where(source_rows == NB - 1, -inhib_gain, 1.0).astype(jnp.float32)
    return (factor * magnitude * signs[:, None, None]).astype(jnp.bfloat16)

def to_delays(q_lag, lag_target):
    classes = jnp.arange(LAGS, dtype=jnp.int32)
    target_slot = (classes[:, None] + 2 * lag_target[None, :]) % DELAYS
    hits = target_slot[None, :, :] == jnp.arange(DELAYS, dtype=jnp.int32)[:, None, None]
    return lax.optimization_barrier(jnp.sum(jnp.where(hits, q_lag[None], jnp.zeros((), jnp.float32)), axis=1))

def reference(pattern, target_area, source_block, target_block, neuron_lag, tau_mem, v_init, ext_count):
    edge_count = target_area.shape[0]
    src_dev = jnp.arange(edge_count, dtype=jnp.int32) // OUT_DEV
    src_global = src_dev * NB + source_block
    tgt_global = target_area[:, 0] * NB + target_block
    alpha = jnp.exp(-step_ms / tau_mem)
    lag_rows = neuron_lag.reshape(N_AREA * NB, BLK)
    classes = jnp.arange(LAGS, dtype=jnp.int32)
    due = jnp.zeros((DELAYS, NEURONS), jnp.float32)
    volt = v_init
    records = []
    for step in range(STEPS):
        volt = alpha * volt + due[0] + ext_gain * (ext_count[step].astype(jnp.float32) - 1.5)
        rate = jax.nn.sigmoid(slope * (volt - threshold))
        volt = volt - reset_part * rate
        spikes = rate.astype(jnp.bfloat16)
        records.append(spikes)
        spike_rows = lax.optimization_barrier(spikes).astype(jnp.float32).reshape(N_AREA * NB, BLK)

        def group(q_sum, index):
            begin = (index * OUT_DEV).astype(jnp.int32)
            pat_rows = lax.dynamic_slice_in_dim(pattern, begin, OUT_DEV, 0)
            src_rows = lax.dynamic_slice_in_dim(source_block, begin, OUT_DEV, 0)
            src_ids = lax.dynamic_slice_in_dim(src_global, begin, OUT_DEV, 0)
            tgt_ids = lax.dynamic_slice_in_dim(tgt_global, begin, OUT_DEV, 0)
            weights = lax.optimization_barrier(block_weights(pat_rows, src_rows)).astype(jnp.float32)
            inputs = spike_rows[src_ids]
            lags = lag_rows[src_ids]
            sorted_in = jnp.where(lags[:, None, :] == classes[None, :, None], inputs[:, None, :], jnp.zeros((), jnp.float32))
            terms = jnp.einsum('sci,sij->scj', sorted_in, weights, precision=lax.Precision.HIGHEST)
            return (q_sum.at[tgt_ids].add(terms), None)
        q_sum, _ = lax.scan(group, jnp.zeros((N_AREA * NB, LAGS, BLK), jnp.float32), jnp.arange(N_AREA, dtype=jnp.int32))
        q_lag = q_sum.transpose(1, 0, 2).reshape(LAGS, NEURONS)
        due = jnp.concatenate([due[1:], jnp.zeros((1, NEURONS), jnp.float32)], 0) + to_delays(q_lag, neuron_lag)
    return (volt, jnp.stack(records), due)
```

```python
import functools
import math

import jax
import jax.numpy as jnp
from jax import lax
from jax.experimental import pallas as pl
from jax.experimental.pallas import tpu as pltpu
from jax.sharding import PartitionSpec as P

BLK = 128
NB = 4
DELAYS = 15
ROWS = 16

step_ms = 0.1
ext_gain = 0.25
threshold = 1.0
slope = 4.0
reset_part = 0.5
inhib_gain = 3.0

CHUNKS = 8


def kernel(
    areas,
    edges,
    steps,
    pattern,
    route,
    tgt,
    src,
    lag,
    tau,
    v_init,
    ext,
    volt_out,
    act_out,
    pend_out,
    raw,
    weights,
    hot,
    inputs,
    terms,
    shift,
    q_lag,
    due,
    acts,
    inbox,
    pend_in,
    load_sem,
    send_sem,
    recv_sem,
    fin_send,
    fin_recv,
):
    me = lax.axis_index("area")
    local = NB * BLK
    targets = NB * areas
    per = edges // CHUNKS

    def load(k):
        return pltpu.make_async_copy(
            pattern.at[pl.ds(k * per, per)], raw.at[pl.ds(k * per, per)], load_sem.at[k]
        )

    for k in range(CHUNKS):
        load(k).start()

    barrier = pltpu.get_barrier_semaphore()

    def greet(k, carry):
        peer = lax.rem(me + k, areas)
        pl.semaphore_signal(
            barrier, inc=1, device_id={"area": peer}, device_id_type=pl.DeviceIdType.MESH
        )
        return carry

    lax.fori_loop(1, areas, greet, 0)

    where_to = route[pl.ds(me, 1), :] + areas * tgt[pl.ds(me, 1), :]
    ids = lax.broadcasted_iota(jnp.int32, (targets, edges), 0)
    one_hot = (ids == where_to).astype(jnp.float32).astype(jnp.bfloat16)
    hot[:, :edges] = one_hot
    hot[:, edges:] = one_hot
    for b in range(NB):
        turned = 2 * lag[pl.ds(b, areas, stride=NB), :]
        turned = jnp.where(turned >= DELAYS, turned - DELAYS, turned)
        turned = jnp.where(turned >= DELAYS, turned - DELAYS, turned)
        shift[pl.ds(b * areas, areas), :] = turned
    due[...] = jnp.zeros_like(due)
    own_class = []
    for b in range(NB):
        row = lag[pl.ds(me * NB + b, 1), :]
        own_class.append(jnp.where(row >= DELAYS, row - DELAYS, row))
    classes = lax.broadcasted_iota(jnp.int32, (ROWS, BLK), 0)
    alpha = jnp.exp(-step_ms / tau[...])

    factor = 8.0 / math.sqrt(BLK * edges / NB)
    for k in range(CHUNKS):
        load(k).wait()

        def build(n, carry):
            e = k * per + n
            sign = jnp.where(src[me * edges + e] == NB - 1, -inhib_gain, 1.0)
            mag = jnp.maximum(raw[e].astype(jnp.float32) - 999.0, 0.0)
            weights[e] = (mag * (sign * (factor / 1000.0))).astype(jnp.bfloat16)
            return carry

        lax.fori_loop(0, per, build, 0)

    pl.semaphore_wait(barrier, areas - 1)

    def message(t, peer, slot):
        return pltpu.make_async_remote_copy(
            src_ref=due.at[0, pl.ds(peer, 1), :],
            dst_ref=inbox.at[t, pl.ds(me, 1), :],
            send_sem=send_sem.at[slot],
            recv_sem=recv_sem.at[t, me],
            device_id={"area": peer},
            device_id_type=pl.DeviceIdType.MESH,
        )

    def arrival(t, peer):
        return pltpu.make_async_remote_copy(
            src_ref=due.at[0, pl.ds(me, 1), :],
            dst_ref=inbox.at[t, pl.ds(peer, 1), :],
            send_sem=send_sem.at[0],
            recv_sem=recv_sem.at[t, peer],
            device_id={"area": peer},
            device_id_type=pl.DeviceIdType.MESH,
        )

    def step_to(t, volt, arrived):
        volt = alpha * volt + arrived + ext_gain * (ext[pl.ds(t, 1), :].astype(jnp.float32) - 1.5)
        rate = jax.nn.sigmoid(slope * (volt - threshold))
        volt = volt - reset_part * rate
        acts[pl.ds(t, 1), :] = rate
        for b in range(NB):
            part = rate[:, b * BLK : (b + 1) * BLK]
            inputs[b] = jnp.where(classes == own_class[b], part, 0.0).astype(jnp.bfloat16)

        def multiply(e, carry):
            terms[pl.ds(pl.multiple_of(e * ROWS, ROWS), ROWS), :] = jnp.dot(
                inputs[src[me * edges + e]], weights[e], preferred_element_type=jnp.float32
            )
            return carry

        lax.fori_loop(0, edges, multiply, 0, unroll=8)

        for c in range(DELAYS):
            term = terms[pl.ds(c, edges, stride=ROWS), :]
            high = term.astype(jnp.bfloat16)
            low = (term - high.astype(jnp.float32)).astype(jnp.bfloat16)
            q_lag[c] = jnp.dot(
                hot[...],
                jnp.concatenate([high, low], axis=0),
                preferred_element_type=jnp.float32,
            )

        for b in range(NB):
            lanes = pl.ds(b * BLK, BLK)

            def turn(r, carry):
                rows = pl.ds(pl.multiple_of(b * areas + r * 8, 8), 8)
                by = shift[rows, :]
                q = [q_lag[c, rows, :] for c in range(DELAYS)]
                for bit in range(4):
                    on = (by & (1 << bit)) != 0
                    q = [jnp.where(on, q[(m - (1 << bit)) % DELAYS], q[m]) for m in range(DELAYS)]
                to = pl.ds(pl.multiple_of(r * 8, 8), 8)
                for m in range(DELAYS):
                    old = due[m + 1, to, lanes] if m < DELAYS - 1 else 0.0
                    due[m, to, lanes] = old + q[m]
                return carry

            lax.fori_loop(0, areas // 8, turn, 0)
        return volt

    def one_step(t, volt):
        def send(k, carry):
            message(t, lax.rem(me + k, areas), k).start()
            return carry

        def receive(k, carry):
            arrival(t, lax.rem(me + k, areas)).wait_recv()
            return carry

        def sent(k, carry):
            message(t, lax.rem(me + k, areas), k).wait_send()
            return carry

        lax.fori_loop(1, areas, send, 0)
        inbox[t, pl.ds(me, 1), :] = due[0, pl.ds(me, 1), :]
        lax.fori_loop(1, areas, receive, 0)
        lax.fori_loop(1, areas, sent, 0)
        arrived = jnp.sum(inbox[t], axis=0, keepdims=True)
        return step_to(t + 1, volt, arrived)

    volt = step_to(0, v_init[...], 0.0)
    volt = lax.fori_loop(0, steps - 1, one_step, volt)

    def final(peer, slot):
        return pltpu.make_async_remote_copy(
            src_ref=due.at[:, pl.ds(peer, 1), :],
            dst_ref=pend_in.at[:, pl.ds(me, 1), :],
            send_sem=fin_send.at[slot],
            recv_sem=fin_recv.at[me],
            device_id={"area": peer},
            device_id_type=pl.DeviceIdType.MESH,
        )

    def final_from(peer):
        return pltpu.make_async_remote_copy(
            src_ref=due.at[:, pl.ds(me, 1), :],
            dst_ref=pend_in.at[:, pl.ds(peer, 1), :],
            send_sem=fin_send.at[0],
            recv_sem=fin_recv.at[peer],
            device_id={"area": peer},
            device_id_type=pl.DeviceIdType.MESH,
        )

    def send_final(k, carry):
        final(lax.rem(me + k, areas), k).start()
        return carry

    def receive_final(k, carry):
        final_from(lax.rem(me + k, areas)).wait_recv()
        return carry

    def sent_final(k, carry):
        final(lax.rem(me + k, areas), k).wait_send()
        return carry

    lax.fori_loop(1, areas, send_final, 0)
    volt_out[...] = volt
    act_out[...] = acts[pl.ds(0, steps), :].astype(jnp.bfloat16)
    for m in range(DELAYS):
        pend_in[m, pl.ds(me, 1), :] = due[m, pl.ds(me, 1), :]
    lax.fori_loop(1, areas, receive_final, 0)
    for m in range(DELAYS):
        pend_out[pl.ds(m, 1), :] = jnp.sum(pend_in[m], axis=0, keepdims=True)
    lax.fori_loop(1, areas, sent_final, 0)


def body(pattern, target_area, source_block, target_block, neuron_lag, tau_mem, v_init, ext_count):
    areas = lax.axis_size("area")
    edges = pattern.shape[0]
    steps, local = ext_count.shape
    vmem = pl.BlockSpec(memory_space=pltpu.VMEM)
    targets = areas * NB
    volt, act, pend = pl.pallas_call(
        functools.partial(kernel, areas, edges, steps),
        out_shape=(
            jax.ShapeDtypeStruct((1, local), jnp.float32),
            jax.ShapeDtypeStruct((steps, local), jnp.bfloat16),
            jax.ShapeDtypeStruct((DELAYS, local), jnp.float32),
        ),
        in_specs=[
            pl.BlockSpec(memory_space=pl.ANY),
            vmem,
            vmem,
            pl.BlockSpec(memory_space=pltpu.SMEM),
            vmem,
            vmem,
            vmem,
            vmem,
        ],
        out_specs=(vmem, vmem, vmem),
        scratch_shapes=[
            pltpu.VMEM((edges, BLK, BLK), jnp.int32),
            pltpu.VMEM((edges, BLK, BLK), jnp.bfloat16),
            pltpu.VMEM((targets, 2 * edges), jnp.bfloat16),
            pltpu.VMEM((NB, ROWS, BLK), jnp.bfloat16),
            pltpu.VMEM((edges * ROWS, BLK), jnp.float32),
            pltpu.VMEM((targets, BLK), jnp.int32),
            pltpu.VMEM((DELAYS, targets, BLK), jnp.float32),
            pltpu.VMEM((DELAYS, areas, local), jnp.float32),
            pltpu.VMEM((16, local), jnp.float32),
            pltpu.VMEM((steps - 1, areas, local), jnp.float32),
            pltpu.VMEM((DELAYS, areas, local), jnp.float32),
            pltpu.SemaphoreType.DMA((CHUNKS,)),
            pltpu.SemaphoreType.DMA((areas,)),
            pltpu.SemaphoreType.DMA((steps - 1, areas)),
            pltpu.SemaphoreType.DMA((areas,)),
            pltpu.SemaphoreType.DMA((areas,)),
        ],
        compiler_params=pltpu.CompilerParams(
            collective_id=0, has_side_effects=True, vmem_limit_bytes=48 * 1024 * 1024
        ),
    )(
        pattern,
        target_area.reshape(areas, edges),
        target_block.reshape(areas, edges),
        source_block,
        neuron_lag.reshape(targets, BLK),
        tau_mem.reshape(1, local),
        v_init.reshape(1, local),
        ext_count,
    )
    return (volt.reshape(local), act, pend)


def solution(mesh):
    in_specs = (
        P("area", None, None),
        P(),
        P(),
        P(),
        P(),
        P("area"),
        P(("run", "area")),
        P(None, ("run", "area")),
    )
    out_specs = (P(("run", "area")), P(None, ("run", "area")), P(None, ("run", "area")))
    return jax.shard_map(body, mesh=mesh, in_specs=in_specs, out_specs=out_specs, check_vma=False)
```

```python
import functools
import math

import jax
import jax.numpy as jnp
from jax import lax
from jax.experimental import pallas as pl
from jax.experimental.pallas import tpu as pltpu
from jax.sharding import PartitionSpec as P

BLK = 128
NB = 4
DELAYS = 15
ROWS = 16

step_ms = 0.1
ext_gain = 0.25
threshold = 1.0
slope = 4.0
reset_part = 0.5
inhib_gain = 3.0

CHUNKS = 8


def side_by_side(x):
    return jnp.concatenate([x[b : b + 1, :] for b in range(NB)], axis=1)


def stacked(x):
    return jnp.concatenate([x[:, b * BLK : (b + 1) * BLK] for b in range(NB)], axis=0)


def split(x):
    high = x.astype(jnp.bfloat16)
    low = (x - high.astype(jnp.float32)).astype(jnp.bfloat16)
    return jnp.concatenate([high, low], axis=0)


def kernel(
    areas,
    edges,
    steps,
    pattern,
    route_in,
    tgt_in,
    src_in,
    lag_in,
    tau_in,
    v_in,
    ext_in,
    volt_out,
    act_out,
    pend_out,
    raw,
    weights,
    route,
    tgt,
    src,
    lag,
    tau,
    v_init,
    ext,
    hot,
    inputs,
    terms,
    shift,
    first,
    drive,
    q_lag,
    due,
    acts,
    outbox,
    inbox,
    pend_go,
    pend_in,
    small_sem,
    load_sem,
    send_sem,
    recv_sem,
    fin_send,
    fin_recv,
):
    me = lax.axis_index("area")
    targets = NB * areas
    per = edges // CHUNKS

    small = [
        pltpu.make_async_copy(a, b, small_sem.at[k])
        for k, (a, b) in enumerate(
            [
                (src_in, src),
                (lag_in, lag),
                (route_in, route),
                (tgt_in, tgt),
                (tau_in, tau),
                (v_in, v_init),
                (ext_in, ext),
            ]
        )
    ]
    for copy in small:
        copy.start()

    def load(k):
        return pltpu.make_async_copy(
            pattern.at[pl.ds(k * per, per)], raw.at[pl.ds(k * per, per)], load_sem.at[k]
        )

    for k in range(CHUNKS):
        load(k).start()

    def peer_at(k):
        p = me + k
        return jnp.where(p >= areas, p - areas, p)

    def every_peer(act):
        if areas <= 16:
            for k in sorted(range(1, areas), key=lambda k: abs(2 * k - areas)):
                act(peer_at(k))
        else:

            def one(k, carry):
                act(peer_at(k))
                return carry

            lax.fori_loop(1, areas, one, 0)

    barrier = pltpu.get_barrier_semaphore()

    def greet(peer):
        pl.semaphore_signal(
            barrier, inc=1, device_id={"area": peer}, device_id_type=pl.DeviceIdType.MESH
        )

    every_peer(greet)
    for copy in small:
        copy.wait()

    where_to = NB * route[pl.ds(me, 1), :] + tgt[pl.ds(me, 1), :]
    ids = lax.broadcasted_iota(jnp.int32, (targets, edges), 0)
    one_hot = (ids == where_to).astype(jnp.float32).astype(jnp.bfloat16)
    hot[:, :edges] = one_hot
    hot[:, edges:] = one_hot
    turned = 2 * lag[...]
    turned = jnp.where(turned >= DELAYS, turned - DELAYS, turned)
    turned = jnp.where(turned >= DELAYS, turned - DELAYS, turned)
    shift[...] = turned
    at_once = jnp.where(turned == 0, 0, DELAYS - turned)
    first[...] = lax.dot_general(
        one_hot,
        at_once.astype(jnp.float32).astype(jnp.bfloat16),
        (((0,), (0,)), ((), ())),
        preferred_element_type=jnp.float32,
    )
    due[...] = jnp.zeros_like(due)
    own_class = []
    for b in range(NB):
        row = lag[pl.ds(me * NB + b, 1), :]
        own_class.append(jnp.where(row >= DELAYS, row - DELAYS, row))
    classes = lax.broadcasted_iota(jnp.int32, (ROWS, BLK), 0)
    alpha = jnp.exp(-step_ms / stacked(tau[...]))
    for t in range(steps):
        drive[t] = ext_gain * (stacked(ext[pl.ds(t, 1), :]).astype(jnp.float32) - 1.5)

    factor = 8.0 / math.sqrt(BLK * edges / NB)
    for k in range(CHUNKS):
        load(k).wait()

        def build(n, carry):
            g = k * (per // 2) + n
            for half in range(2):
                e = 2 * g + half
                sign = jnp.where(src[me * edges + e] == NB - 1, -inhib_gain, 1.0)
                mag = jnp.maximum(raw[e].astype(jnp.float32) - 999.0, 0.0)
                weights[g, pl.ds(half * BLK, BLK), :] = (mag * (sign * (factor / 1000.0))).astype(
                    jnp.bfloat16
                )
            return carry

        lax.fori_loop(0, per // 2, build, 0)

    def think(t, volt, arrived):
        volt = alpha * volt + arrived + drive[t]
        rate = jax.nn.sigmoid(slope * (volt - threshold))
        volt = volt - reset_part * rate
        for b in range(NB):
            inputs[b] = jnp.where(classes == own_class[b], rate[b : b + 1, :], 0.0).astype(
                jnp.bfloat16
            )
        none = jnp.zeros((ROWS, BLK), jnp.bfloat16)

        def multiply(g, carry):
            upper = inputs[src[me * edges + 2 * g]]
            lower = inputs[src[me * edges + 2 * g + 1]]
            both = jnp.concatenate(
                [
                    jnp.concatenate([upper, none], axis=1),
                    jnp.concatenate([none, lower], axis=1),
                ],
                axis=0,
            )
            rows = pl.ds(pl.multiple_of(g * (2 * ROWS), 2 * ROWS), 2 * ROWS)
            terms[rows, :] = jnp.dot(both, weights[g], preferred_element_type=jnp.float32)
            return carry

        lax.fori_loop(0, edges // 2, multiply, 0, unroll=32)
        return volt, rate

    def gather_lags():
        for c in range(DELAYS):
            q_lag[c] = jnp.dot(
                hot[...],
                split(terms[pl.ds(c, edges, stride=ROWS), :]),
                preferred_element_type=jnp.float32,
            )

    def arrivals(rows):
        by = shift[rows, :]
        q = [q_lag[c, rows, :] for c in range(DELAYS)]
        for bit in range(4):
            on = (by & (1 << bit)) != 0
            q = [jnp.where(on, q[(m - (1 << bit)) % DELAYS], q[m]) for m in range(DELAYS)]
        for m in range(DELAYS - 1):
            q[m] = q[m] + due[m + 1, rows, :]
        return q

    def one_step(t, carry):
        volt, arrived = carry
        volt, rate = think(t, volt, arrived)
        picked = []
        for e in range(0, edges, 32):
            mine = first[pl.ds(e, 32), :]
            y = jnp.zeros((32, BLK), jnp.float32)
            for c in range(DELAYS):
                y = jnp.where(mine == float(c), terms[pl.ds(e * ROWS + c, 32, stride=ROWS), :], y)
            picked.append(y)
        soon = due[1] + jnp.dot(
            hot[...], split(jnp.concatenate(picked, axis=0)), preferred_element_type=jnp.float32
        )
        for a in range(areas):
            outbox[t, a] = soon[a * NB : (a + 1) * NB, :]

        def send(peer):
            pltpu.make_async_remote_copy(
                src_ref=outbox.at[t, peer],
                dst_ref=inbox.at[t, me],
                send_sem=send_sem.at[t],
                recv_sem=recv_sem.at[t],
                device_id={"area": peer},
                device_id_type=pl.DeviceIdType.MESH,
            ).start()

        every_peer(send)
        inbox[t, me] = outbox[t, me]
        acts[pl.ds(t, 1), :] = side_by_side(rate)
        gather_lags()

        def turn(r, carry):
            rows = pl.ds(pl.multiple_of(r * 8, 8), 8)
            q = arrivals(rows)
            for m in range(DELAYS):
                due[m, rows, :] = q[m]
            return carry

        lax.fori_loop(0, targets // 8, turn, 0)
        step_messages(t).wait_recv()
        return volt, jnp.sum(inbox[t], axis=0)

    def step_messages(t):
        return pltpu.make_async_remote_copy(
            src_ref=outbox.at[t, pl.ds(0, areas - 1)],
            dst_ref=inbox.at[t, pl.ds(0, areas - 1)],
            send_sem=send_sem.at[t],
            recv_sem=recv_sem.at[t],
            device_id={"area": me},
            device_id_type=pl.DeviceIdType.MESH,
        )

    pl.semaphore_wait(barrier, areas - 1)
    volt, arrived = lax.fori_loop(
        0, steps - 1, one_step, (stacked(v_init[...]), jnp.zeros((NB, BLK), jnp.float32))
    )
    volt, rate = think(steps - 1, volt, arrived)
    gather_lags()

    def last(n, carry):
        r = n + me // 2 + 1
        r = jnp.where(r >= areas // 2, r - areas // 2, r)
        q = arrivals(pl.ds(pl.multiple_of(r * 8, 8), 8))
        for half in range(2):
            peer = 2 * r + half
            for m in range(DELAYS):
                pend_go[peer, m] = q[m][half * NB : (half + 1) * NB, :]

            @pl.when(peer != me)
            def _():
                pltpu.make_async_remote_copy(
                    src_ref=pend_go.at[peer],
                    dst_ref=pend_in.at[me],
                    send_sem=fin_send,
                    recv_sem=fin_recv,
                    device_id={"area": peer},
                    device_id_type=pl.DeviceIdType.MESH,
                ).start()

        return carry

    lax.fori_loop(0, areas // 2, last, 0)
    acts[pl.ds(steps - 1, 1), :] = side_by_side(rate)
    pend_in[me] = pend_go[me]
    volt_out[...] = side_by_side(volt)
    act_out[...] = acts[pl.ds(0, steps), :].astype(jnp.bfloat16)
    for t in range(steps - 1):
        step_messages(t).wait_send()
    everything = pltpu.make_async_remote_copy(
        src_ref=pend_go.at[pl.ds(0, areas - 1)],
        dst_ref=pend_in.at[pl.ds(0, areas - 1)],
        send_sem=fin_send,
        recv_sem=fin_recv,
        device_id={"area": me},
        device_id_type=pl.DeviceIdType.MESH,
    )
    everything.wait_recv()
    for m in range(DELAYS):
        pend_out[pl.ds(m, 1), :] = side_by_side(jnp.sum(pend_in[:, m], axis=0))
    everything.wait_send()


def body(pattern, target_area, source_block, target_block, neuron_lag, tau_mem, v_init, ext_count):
    areas = lax.axis_size("area")
    edges = pattern.shape[0]
    steps, local = ext_count.shape
    vmem = pl.BlockSpec(memory_space=pltpu.VMEM)
    hbm = pl.BlockSpec(memory_space=pltpu.HBM)
    targets = areas * NB
    f32 = jnp.float32
    volt, act, pend = pl.pallas_call(
        functools.partial(kernel, areas, edges, steps),
        out_shape=(
            jax.ShapeDtypeStruct((1, local), f32),
            jax.ShapeDtypeStruct((steps, local), jnp.bfloat16),
            jax.ShapeDtypeStruct((DELAYS, local), f32),
        ),
        in_specs=[hbm] * 8,
        out_specs=(vmem, vmem, vmem),
        scratch_shapes=[
            pltpu.VMEM((edges, BLK, BLK), jnp.int32),
            pltpu.VMEM((edges // 2, 2 * BLK, BLK), jnp.bfloat16),
            pltpu.VMEM((areas, edges), jnp.int32),
            pltpu.VMEM((areas, edges), jnp.int32),
            pltpu.SMEM((areas * edges,), jnp.int32),
            pltpu.VMEM((targets, BLK), jnp.int32),
            pltpu.VMEM((1, local), f32),
            pltpu.VMEM((1, local), f32),
            pltpu.VMEM((steps, local), jnp.int32),
            pltpu.VMEM((targets, 2 * edges), jnp.bfloat16),
            pltpu.VMEM((NB, ROWS, BLK), jnp.bfloat16),
            pltpu.VMEM((edges * ROWS, BLK), f32),
            pltpu.VMEM((targets, BLK), jnp.int32),
            pltpu.VMEM((edges, BLK), f32),
            pltpu.VMEM((steps, NB, BLK), f32),
            pltpu.VMEM((DELAYS, targets, BLK), f32),
            pltpu.VMEM((DELAYS, targets, BLK), f32),
            pltpu.VMEM((16, local), f32),
            pltpu.VMEM((steps - 1, areas, NB, BLK), f32),
            pltpu.VMEM((steps - 1, areas, NB, BLK), f32),
            pltpu.VMEM((areas, DELAYS, NB, BLK), f32),
            pltpu.VMEM((areas, DELAYS, NB, BLK), f32),
            pltpu.SemaphoreType.DMA((7,)),
            pltpu.SemaphoreType.DMA((CHUNKS,)),
            pltpu.SemaphoreType.DMA((steps - 1,)),
            pltpu.SemaphoreType.DMA((steps - 1,)),
            pltpu.SemaphoreType.DMA,
            pltpu.SemaphoreType.DMA,
        ],
        compiler_params=pltpu.CompilerParams(
            collective_id=0, has_side_effects=True, vmem_limit_bytes=48 * 1024 * 1024
        ),
    )(
        pattern,
        target_area.reshape(areas, edges),
        target_block.reshape(areas, edges),
        source_block,
        neuron_lag.reshape(targets, BLK),
        tau_mem.reshape(1, local),
        v_init.reshape(1, local),
        ext_count,
    )
    return (volt.reshape(local), act, pend)


def solution(mesh):
    in_specs = (
        P("area", None, None),
        P(),
        P(),
        P(),
        P(),
        P("area"),
        P(("run", "area")),
        P(None, ("run", "area")),
    )
    out_specs = (P(("run", "area")), P(None, ("run", "area")), P(None, ("run", "area")))
    return jax.shard_map(body, mesh=mesh, in_specs=in_specs, out_specs=out_specs, check_vma=False)
```

```python
import functools
import math

import jax
import jax.numpy as jnp
from jax import lax
from jax.experimental import pallas as pl
from jax.experimental.pallas import tpu as pltpu
from jax.sharding import PartitionSpec as P

BLK = 128
NB = 4
DELAYS = 15
ROWS = 16

step_ms = 0.1
ext_gain = 0.25
threshold = 1.0
slope = 4.0
reset_part = 0.5
inhib_gain = 3.0

CHUNKS = 8
SHARE = ROWS * NB


def side_by_side(x):
    return jnp.concatenate([x[b : b + 1, :] for b in range(NB)], axis=1)


def stacked(x):
    return jnp.concatenate([x[:, b * BLK : (b + 1) * BLK] for b in range(NB)], axis=0)


def split(x):
    high = x.astype(jnp.bfloat16)
    low = (x - high.astype(jnp.float32)).astype(jnp.bfloat16)
    return jnp.concatenate([high, low], axis=0)


def kernel(
    areas,
    edges,
    steps,
    pattern,
    route_in,
    tgt_in,
    src_in,
    lag_in,
    tau_in,
    v_in,
    ext_in,
    volt_out,
    act_out,
    pend_out,
    raw,
    weights,
    route,
    tgt,
    src,
    lag,
    tau,
    v_init,
    ext,
    hot,
    inputs,
    terms,
    shift,
    first,
    drive,
    q_lag,
    due,
    acts,
    outbox,
    inbox,
    pend_go,
    pend_in,
    small_sem,
    load_sem,
    send_sem,
    recv_sem,
    fin_send,
    fin_recv,
):
    me = lax.axis_index("area")
    targets = NB * areas
    per = edges // CHUNKS

    small = [
        pltpu.make_async_copy(a, b, small_sem.at[k])
        for k, (a, b) in enumerate(
            [
                (src_in, src),
                (lag_in, lag),
                (route_in, route),
                (tgt_in, tgt),
                (tau_in, tau),
                (v_in, v_init),
                (ext_in, ext),
            ]
        )
    ]
    for copy in small:
        copy.start()

    def load(k):
        return pltpu.make_async_copy(
            pattern.at[pl.ds(k * per, per)], raw.at[pl.ds(k * per, per)], load_sem.at[k]
        )

    for k in range(CHUNKS):
        load(k).start()

    def peer_at(k):
        p = me + k
        return jnp.where(p >= areas, p - areas, p)

    def every_peer(act):
        if areas <= 16:
            for k in sorted(range(1, areas), key=lambda k: abs(2 * k - areas)):
                act(peer_at(k))
        else:

            def one(k, carry):
                act(peer_at(k))
                return carry

            lax.fori_loop(1, areas, one, 0)

    barrier = pltpu.get_barrier_semaphore()

    def greet(peer):
        pl.semaphore_signal(
            barrier, inc=1, device_id={"area": peer}, device_id_type=pl.DeviceIdType.MESH
        )

    every_peer(greet)
    for copy in small:
        copy.wait()

    where_to = NB * route[pl.ds(me, 1), :] + tgt[pl.ds(me, 1), :]
    ids = lax.broadcasted_iota(jnp.int32, (targets, edges), 0)
    one_hot = (ids == where_to).astype(jnp.float32).astype(jnp.bfloat16)
    hot[:, :edges] = one_hot
    hot[:, edges:] = one_hot
    turned = 2 * lag[...]
    turned = jnp.where(turned >= DELAYS, turned - DELAYS, turned)
    turned = jnp.where(turned >= DELAYS, turned - DELAYS, turned)
    shift[...] = turned
    at_once = jnp.where(turned == 0, 0, DELAYS - turned)
    first[...] = lax.dot_general(
        one_hot,
        at_once.astype(jnp.float32).astype(jnp.bfloat16),
        (((0,), (0,)), ((), ())),
        preferred_element_type=jnp.float32,
    )
    due[...] = jnp.zeros_like(due)
    own_class = []
    for b in range(NB):
        row = lag[pl.ds(me * NB + b, 1), :]
        own_class.append(jnp.where(row >= DELAYS, row - DELAYS, row))
    classes = lax.broadcasted_iota(jnp.int32, (ROWS, BLK), 0)
    alpha = jnp.exp(-step_ms / stacked(tau[...]))
    for t in range(steps):
        drive[t] = ext_gain * (stacked(ext[pl.ds(t, 1), :]).astype(jnp.float32) - 1.5)

    factor = 8.0 / math.sqrt(BLK * edges / NB)
    for k in range(CHUNKS):
        load(k).wait()

        def build(n, carry):
            g = k * (per // 2) + n
            for half in range(2):
                e = 2 * g + half
                sign = jnp.where(src[me * edges + e] == NB - 1, -inhib_gain, 1.0)
                mag = jnp.maximum(raw[e].astype(jnp.float32) - 999.0, 0.0)
                weights[g, pl.ds(half * BLK, BLK), :] = (mag * (sign * (factor / 1000.0))).astype(
                    jnp.bfloat16
                )
            return carry

        lax.fori_loop(0, per // 2, build, 0)

    def think(t, volt, arrived):
        volt = alpha * volt + arrived + drive[t]
        rate = jax.nn.sigmoid(slope * (volt - threshold))
        volt = volt - reset_part * rate
        for b in range(NB):
            inputs[b] = jnp.where(classes == own_class[b], rate[b : b + 1, :], 0.0).astype(
                jnp.bfloat16
            )
        none = jnp.zeros((ROWS, BLK), jnp.bfloat16)

        def multiply(g, carry):
            upper = inputs[src[me * edges + 2 * g]]
            lower = inputs[src[me * edges + 2 * g + 1]]
            both = jnp.concatenate(
                [
                    jnp.concatenate([upper, none], axis=1),
                    jnp.concatenate([none, lower], axis=1),
                ],
                axis=0,
            )
            rows = pl.ds(pl.multiple_of(g * (2 * ROWS), 2 * ROWS), 2 * ROWS)
            terms[rows, :] = jnp.dot(both, weights[g], preferred_element_type=jnp.float32)
            return carry

        lax.fori_loop(0, edges // 2, multiply, 0, unroll=64 if areas <= 16 else 32)
        return volt, rate

    def gather_lags():
        for c in range(DELAYS):
            q_lag[c] = jnp.dot(
                hot[...],
                split(terms[pl.ds(c, edges, stride=ROWS), :]),
                preferred_element_type=jnp.float32,
            )

    def arrivals(rows):
        by = shift[rows, :]
        q = [q_lag[c, rows, :] for c in range(DELAYS)]
        for bit in range(4):
            on = (by & (1 << bit)) != 0
            q = [jnp.where(on, q[(m - (1 << bit)) % DELAYS], q[m]) for m in range(DELAYS)]
        for m in range(DELAYS - 1):
            q[m] = q[m] + due[m + 1, rows, :]
        return q

    def one_step(t, carry):
        volt, arrived = carry
        volt, rate = think(t, volt, arrived)
        picked = []
        for e in range(0, edges, 32):
            mine = first[pl.ds(e, 32), :]
            y = jnp.zeros((32, BLK), jnp.float32)
            for c in range(DELAYS):
                y = jnp.where(mine == float(c), terms[pl.ds(e * ROWS + c, 32, stride=ROWS), :], y)
            picked.append(y)
        soon = due[1] + jnp.dot(
            hot[...], split(jnp.concatenate(picked, axis=0)), preferred_element_type=jnp.float32
        )
        for a in range(areas):
            outbox[t, a] = soon[a * NB : (a + 1) * NB, :]

        def send(peer):
            pltpu.make_async_remote_copy(
                src_ref=outbox.at[t, peer],
                dst_ref=inbox.at[t, me],
                send_sem=send_sem.at[t],
                recv_sem=recv_sem.at[t],
                device_id={"area": peer},
                device_id_type=pl.DeviceIdType.MESH,
            ).start()

        every_peer(send)
        inbox[t, me] = outbox[t, me]
        acts[pl.ds(t, 1), :] = side_by_side(rate)
        gather_lags()

        def turn(r, carry):
            rows = pl.ds(pl.multiple_of(r * 8, 8), 8)
            q = arrivals(rows)
            for m in range(DELAYS):
                due[m, rows, :] = q[m]
            return carry

        lax.fori_loop(0, targets // 8, turn, 0)
        step_messages(t).wait_recv()
        return volt, jnp.sum(inbox[t], axis=0)

    def step_messages(t):
        return pltpu.make_async_remote_copy(
            src_ref=outbox.at[t, pl.ds(0, areas - 1)],
            dst_ref=inbox.at[t, pl.ds(0, areas - 1)],
            send_sem=send_sem.at[t],
            recv_sem=recv_sem.at[t],
            device_id={"area": me},
            device_id_type=pl.DeviceIdType.MESH,
        )

    pl.semaphore_wait(barrier, areas - 1)
    volt, arrived = lax.fori_loop(
        0, steps - 1, one_step, (stacked(v_init[...]), jnp.zeros((NB, BLK), jnp.float32))
    )
    volt, rate = think(steps - 1, volt, arrived)
    gather_lags()

    def share(a):
        return pl.ds(pl.multiple_of(a * SHARE, SHARE), SHARE)

    def last(n, carry):
        r = n + me // 2 + 1
        r = jnp.where(r >= areas // 2, r - areas // 2, r)
        q = arrivals(pl.ds(pl.multiple_of(r * 8, 8), 8))
        for half in range(2):
            peer = 2 * r + half
            parts = [q[m][half * NB : (half + 1) * NB, :] for m in range(DELAYS)]
            parts.append(jnp.zeros((NB, BLK), jnp.float32))
            pend_go[share(peer), :] = jnp.concatenate(parts, axis=0).astype(jnp.bfloat16)

            @pl.when(peer != me)
            def _():
                pltpu.make_async_remote_copy(
                    src_ref=pend_go.at[share(peer)],
                    dst_ref=pend_in.at[share(me)],
                    send_sem=fin_send,
                    recv_sem=fin_recv,
                    device_id={"area": peer},
                    device_id_type=pl.DeviceIdType.MESH,
                ).start()

        return carry

    lax.fori_loop(0, areas // 2, last, 0)
    acts[pl.ds(steps - 1, 1), :] = side_by_side(rate)
    pend_in[share(me), :] = pend_go[share(me), :]
    volt_out[...] = side_by_side(volt)
    act_out[...] = acts[pl.ds(0, steps), :].astype(jnp.bfloat16)
    for t in range(steps - 1):
        step_messages(t).wait_send()
    everything = pltpu.make_async_remote_copy(
        src_ref=pend_go.at[pl.ds(0, (areas - 1) * SHARE)],
        dst_ref=pend_in.at[pl.ds(0, (areas - 1) * SHARE)],
        send_sem=fin_send,
        recv_sem=fin_recv,
        device_id={"area": me},
        device_id_type=pl.DeviceIdType.MESH,
    )
    everything.wait_recv()
    total = jnp.zeros((SHARE, BLK), jnp.float32)
    for a in range(areas):
        total = total + pend_in[pl.ds(a * SHARE, SHARE), :].astype(jnp.float32)
    for m in range(DELAYS):
        pend_out[pl.ds(m, 1), :] = side_by_side(total[m * NB : (m + 1) * NB, :])
    everything.wait_send()


def body(pattern, target_area, source_block, target_block, neuron_lag, tau_mem, v_init, ext_count):
    areas = lax.axis_size("area")
    edges = pattern.shape[0]
    steps, local = ext_count.shape
    vmem = pl.BlockSpec(memory_space=pltpu.VMEM)
    hbm = pl.BlockSpec(memory_space=pltpu.HBM)
    targets = areas * NB
    f32 = jnp.float32
    volt, act, pend = pl.pallas_call(
        functools.partial(kernel, areas, edges, steps),
        out_shape=(
            jax.ShapeDtypeStruct((1, local), f32),
            jax.ShapeDtypeStruct((steps, local), jnp.bfloat16),
            jax.ShapeDtypeStruct((DELAYS, local), f32),
        ),
        in_specs=[hbm] * 8,
        out_specs=(vmem, vmem, vmem),
        scratch_shapes=[
            pltpu.VMEM((edges, BLK, BLK), jnp.int32),
            pltpu.VMEM((edges // 2, 2 * BLK, BLK), jnp.bfloat16),
            pltpu.VMEM((areas, edges), jnp.int32),
            pltpu.VMEM((areas, edges), jnp.int32),
            pltpu.SMEM((areas * edges,), jnp.int32),
            pltpu.VMEM((targets, BLK), jnp.int32),
            pltpu.VMEM((1, local), f32),
            pltpu.VMEM((1, local), f32),
            pltpu.VMEM((steps, local), jnp.int32),
            pltpu.VMEM((targets, 2 * edges), jnp.bfloat16),
            pltpu.VMEM((NB, ROWS, BLK), jnp.bfloat16),
            pltpu.VMEM((edges * ROWS, BLK), f32),
            pltpu.VMEM((targets, BLK), jnp.int32),
            pltpu.VMEM((edges, BLK), f32),
            pltpu.VMEM((steps, NB, BLK), f32),
            pltpu.VMEM((DELAYS, targets, BLK), f32),
            pltpu.VMEM((DELAYS, targets, BLK), f32),
            pltpu.VMEM((16, local), f32),
            pltpu.VMEM((steps - 1, areas, NB, BLK), f32),
            pltpu.VMEM((steps - 1, areas, NB, BLK), f32),
            pltpu.VMEM((areas * SHARE, BLK), jnp.bfloat16),
            pltpu.VMEM((areas * SHARE, BLK), jnp.bfloat16),
            pltpu.SemaphoreType.DMA((7,)),
            pltpu.SemaphoreType.DMA((CHUNKS,)),
            pltpu.SemaphoreType.DMA((steps - 1,)),
            pltpu.SemaphoreType.DMA((steps - 1,)),
            pltpu.SemaphoreType.DMA,
            pltpu.SemaphoreType.DMA,
        ],
        compiler_params=pltpu.CompilerParams(
            collective_id=0, has_side_effects=True, vmem_limit_bytes=48 * 1024 * 1024
        ),
    )(
        pattern,
        target_area.reshape(areas, edges),
        target_block.reshape(areas, edges),
        source_block,
        neuron_lag.reshape(targets, BLK),
        tau_mem.reshape(1, local),
        v_init.reshape(1, local),
        ext_count,
    )
    return (volt.reshape(local), act, pend)


def solution(mesh):
    in_specs = (
        P("area", None, None),
        P(),
        P(),
        P(),
        P(),
        P("area"),
        P(("run", "area")),
        P(None, ("run", "area")),
    )
    out_specs = (P(("run", "area")), P(None, ("run", "area")), P(None, ("run", "area")))
    return jax.shard_map(body, mesh=mesh, in_specs=in_specs, out_specs=out_specs, check_vma=False)
```

```python
import functools
import math

import jax
import jax.numpy as jnp
from jax import lax
from jax.experimental import pallas as pl
from jax.experimental.pallas import tpu as pltpu
from jax.sharding import PartitionSpec as P

BLK = 128
NB = 4
DELAYS = 15
ROWS = 16

step_ms = 0.1
ext_gain = 0.25
threshold = 1.0
slope = 4.0
reset_part = 0.5
inhib_gain = 3.0

CHUNKS = 8
SHARE = ROWS * NB


def side_by_side(x):
    return jnp.concatenate([x[b : b + 1, :] for b in range(NB)], axis=1)


def stacked(x):
    return jnp.concatenate([x[:, b * BLK : (b + 1) * BLK] for b in range(NB)], axis=0)


def split(x):
    high = x.astype(jnp.bfloat16)
    low = (x - high.astype(jnp.float32)).astype(jnp.bfloat16)
    return jnp.concatenate([high, low], axis=0)


def kernel(
    areas,
    edges,
    steps,
    pattern,
    route_in,
    tgt_in,
    src_in,
    lag_in,
    tau_in,
    v_in,
    ext_in,
    volt_out,
    act_out,
    pend_out,
    raw,
    weights,
    route,
    tgt,
    src,
    lag,
    tau,
    v_init,
    ext,
    hot,
    inputs,
    terms,
    shift,
    first,
    drive,
    q_lag,
    due,
    acts,
    outbox,
    inbox,
    pend_go,
    pend_in,
    small_sem,
    load_sem,
    send_sem,
    recv_sem,
    fin_send,
    fin_recv,
):
    me = lax.axis_index("area")
    targets = NB * areas
    per = edges // CHUNKS

    small = [
        pltpu.make_async_copy(a, b, small_sem.at[k])
        for k, (a, b) in enumerate(
            [
                (src_in, src),
                (lag_in, lag),
                (route_in, route),
                (tgt_in, tgt),
                (tau_in, tau),
                (v_in, v_init),
                (ext_in, ext),
            ]
        )
    ]
    for copy in small:
        copy.start()

    def load(k):
        return pltpu.make_async_copy(
            pattern.at[pl.ds(k * per, per)], raw.at[pl.ds(k * per, per)], load_sem.at[k]
        )

    for k in range(CHUNKS):
        load(k).start()

    def peer_at(k):
        p = me + k
        return jnp.where(p >= areas, p - areas, p)

    def every_peer(act):
        if areas <= 16:
            for k in sorted(range(1, areas), key=lambda k: -abs(2 * k - areas)):
                act(peer_at(k))
        else:

            def one(k, carry):
                act(peer_at(k))
                return carry

            lax.fori_loop(1, areas, one, 0)

    barrier = pltpu.get_barrier_semaphore()

    def greet(peer):
        pl.semaphore_signal(
            barrier, inc=1, device_id={"area": peer}, device_id_type=pl.DeviceIdType.MESH
        )

    every_peer(greet)
    for copy in small:
        copy.wait()

    where_to = NB * route[pl.ds(me, 1), :] + tgt[pl.ds(me, 1), :]
    ids = lax.broadcasted_iota(jnp.int32, (targets, edges), 0)
    one_hot = (ids == where_to).astype(jnp.float32).astype(jnp.bfloat16)
    hot[:, :edges] = one_hot
    hot[:, edges:] = one_hot
    turned = 2 * lag[...]
    turned = jnp.where(turned >= DELAYS, turned - DELAYS, turned)
    turned = jnp.where(turned >= DELAYS, turned - DELAYS, turned)
    shift[...] = turned
    at_once = jnp.where(turned == 0, 0, DELAYS - turned)
    first[...] = lax.dot_general(
        one_hot,
        at_once.astype(jnp.float32).astype(jnp.bfloat16),
        (((0,), (0,)), ((), ())),
        preferred_element_type=jnp.float32,
    )
    due[...] = jnp.zeros_like(due)
    own_class = []
    for b in range(NB):
        row = lag[pl.ds(me * NB + b, 1), :]
        own_class.append(jnp.where(row >= DELAYS, row - DELAYS, row))
    classes = lax.broadcasted_iota(jnp.int32, (ROWS, BLK), 0)
    alpha = jnp.exp(-step_ms / stacked(tau[...]))
    for t in range(steps):
        drive[t] = ext_gain * (stacked(ext[pl.ds(t, 1), :]).astype(jnp.float32) - 1.5)

    factor = 8.0 / math.sqrt(BLK * edges / NB)
    for k in range(CHUNKS):
        load(k).wait()

        def build(n, carry):
            g = k * (per // 2) + n
            for half in range(2):
                e = 2 * g + half
                sign = jnp.where(src[me * edges + e] == NB - 1, -inhib_gain, 1.0)
                mag = jnp.maximum(raw[e].astype(jnp.float32) - 999.0, 0.0)
                weights[g, pl.ds(half * BLK, BLK), :] = (mag * (sign * (factor / 1000.0))).astype(
                    jnp.bfloat16
                )
            return carry

        lax.fori_loop(0, per // 2, build, 0)

    def think(t, volt, arrived):
        volt = alpha * volt + arrived + drive[t]
        rate = jax.nn.sigmoid(slope * (volt - threshold))
        volt = volt - reset_part * rate
        for b in range(NB):
            inputs[b] = jnp.where(classes == own_class[b], rate[b : b + 1, :], 0.0).astype(
                jnp.bfloat16
            )
        none = jnp.zeros((ROWS, BLK), jnp.bfloat16)

        def multiply(g, carry):
            upper = inputs[src[me * edges + 2 * g]]
            lower = inputs[src[me * edges + 2 * g + 1]]
            both = jnp.concatenate(
                [
                    jnp.concatenate([upper, none], axis=1),
                    jnp.concatenate([none, lower], axis=1),
                ],
                axis=0,
            )
            rows = pl.ds(pl.multiple_of(g * (2 * ROWS), 2 * ROWS), 2 * ROWS)
            terms[rows, :] = jnp.dot(both, weights[g], preferred_element_type=jnp.float32)
            return carry

        lax.fori_loop(0, edges // 2, multiply, 0, unroll=64 if areas <= 16 else 32)
        return volt, rate

    def gather_lags():
        for c in range(DELAYS):
            q_lag[c] = jnp.dot(
                hot[...],
                split(terms[pl.ds(c, edges, stride=ROWS), :]),
                preferred_element_type=jnp.float32,
            )

    def arrivals(rows):
        by = shift[rows, :]
        q = [q_lag[c, rows, :] for c in range(DELAYS)]
        for bit in range(4):
            on = (by & (1 << bit)) != 0
            q = [jnp.where(on, q[(m - (1 << bit)) % DELAYS], q[m]) for m in range(DELAYS)]
        for m in range(DELAYS - 1):
            q[m] = q[m] + due[m + 1, rows, :]
        return q

    def one_step(t, carry):
        volt, arrived = carry
        volt, rate = think(t, volt, arrived)
        picked = []
        for e in range(0, edges, 32):
            mine = first[pl.ds(e, 32), :]
            y = jnp.zeros((32, BLK), jnp.float32)
            for c in range(DELAYS):
                y = jnp.where(mine == float(c), terms[pl.ds(e * ROWS + c, 32, stride=ROWS), :], y)
            picked.append(y)
        soon = due[1] + jnp.dot(
            hot[...], split(jnp.concatenate(picked, axis=0)), preferred_element_type=jnp.float32
        )
        for a in range(areas):
            outbox[t, a] = soon[a * NB : (a + 1) * NB, :]

        def send(peer):
            pltpu.make_async_remote_copy(
                src_ref=outbox.at[t, peer],
                dst_ref=inbox.at[t, me],
                send_sem=send_sem.at[t],
                recv_sem=recv_sem.at[t],
                device_id={"area": peer},
                device_id_type=pl.DeviceIdType.MESH,
            ).start()

        every_peer(send)
        inbox[t, me] = outbox[t, me]
        acts[pl.ds(t, 1), :] = side_by_side(rate)
        gather_lags()

        def turn(r, carry):
            rows = pl.ds(pl.multiple_of(r * 8, 8), 8)
            q = arrivals(rows)
            for m in range(DELAYS):
                due[m, rows, :] = q[m]
            return carry

        lax.fori_loop(0, targets // 8, turn, 0)
        step_messages(t).wait_recv()
        return volt, jnp.sum(inbox[t], axis=0)

    def step_messages(t):
        return pltpu.make_async_remote_copy(
            src_ref=outbox.at[t, pl.ds(0, areas - 1)],
            dst_ref=inbox.at[t, pl.ds(0, areas - 1)],
            send_sem=send_sem.at[t],
            recv_sem=recv_sem.at[t],
            device_id={"area": me},
            device_id_type=pl.DeviceIdType.MESH,
        )

    pl.semaphore_wait(barrier, areas - 1)
    volt, arrived = lax.fori_loop(
        0, steps - 1, one_step, (stacked(v_init[...]), jnp.zeros((NB, BLK), jnp.float32))
    )
    volt, rate = think(steps - 1, volt, arrived)
    gather_lags()

    def share(a):
        return pl.ds(pl.multiple_of(a * SHARE, SHARE), SHARE)

    def last(n, carry):
        r = n + me // 2 + 1
        r = jnp.where(r >= areas // 2, r - areas // 2, r)
        q = arrivals(pl.ds(pl.multiple_of(r * 8, 8), 8))
        for half in range(2):
            peer = 2 * r + half
            parts = [q[m][half * NB : (half + 1) * NB, :] for m in range(DELAYS)]
            parts.append(jnp.zeros((NB, BLK), jnp.float32))
            pend_go[share(peer), :] = jnp.concatenate(parts, axis=0).astype(jnp.bfloat16)

            @pl.when(peer != me)
            def _():
                pltpu.make_async_remote_copy(
                    src_ref=pend_go.at[share(peer)],
                    dst_ref=pend_in.at[share(me)],
                    send_sem=fin_send,
                    recv_sem=fin_recv,
                    device_id={"area": peer},
                    device_id_type=pl.DeviceIdType.MESH,
                ).start()

        return carry

    lax.fori_loop(0, areas // 2, last, 0)
    acts[pl.ds(steps - 1, 1), :] = side_by_side(rate)
    pend_in[share(me), :] = pend_go[share(me), :]
    volt_out[...] = side_by_side(volt)
    act_out[...] = acts[pl.ds(0, steps), :].astype(jnp.bfloat16)
    for t in range(steps - 1):
        step_messages(t).wait_send()
    everything = pltpu.make_async_remote_copy(
        src_ref=pend_go.at[pl.ds(0, (areas - 1) * SHARE)],
        dst_ref=pend_in.at[pl.ds(0, (areas - 1) * SHARE)],
        send_sem=fin_send,
        recv_sem=fin_recv,
        device_id={"area": me},
        device_id_type=pl.DeviceIdType.MESH,
    )
    everything.wait_recv()
    total = jnp.zeros((SHARE, BLK), jnp.float32)
    for a in range(areas):
        total = total + pend_in[pl.ds(a * SHARE, SHARE), :].astype(jnp.float32)
    for m in range(DELAYS):
        pend_out[pl.ds(m, 1), :] = side_by_side(total[m * NB : (m + 1) * NB, :])
    everything.wait_send()


def body(pattern, target_area, source_block, target_block, neuron_lag, tau_mem, v_init, ext_count):
    areas = lax.axis_size("area")
    edges = pattern.shape[0]
    steps, local = ext_count.shape
    vmem = pl.BlockSpec(memory_space=pltpu.VMEM)
    hbm = pl.BlockSpec(memory_space=pltpu.HBM)
    targets = areas * NB
    f32 = jnp.float32
    volt, act, pend = pl.pallas_call(
        functools.partial(kernel, areas, edges, steps),
        out_shape=(
            jax.ShapeDtypeStruct((1, local), f32),
            jax.ShapeDtypeStruct((steps, local), jnp.bfloat16),
            jax.ShapeDtypeStruct((DELAYS, local), f32),
        ),
        in_specs=[hbm] * 8,
        out_specs=(vmem, vmem, vmem),
        scratch_shapes=[
            pltpu.VMEM((edges, BLK, BLK), jnp.int32),
            pltpu.VMEM((edges // 2, 2 * BLK, BLK), jnp.bfloat16),
            pltpu.VMEM((areas, edges), jnp.int32),
            pltpu.VMEM((areas, edges), jnp.int32),
            pltpu.SMEM((areas * edges,), jnp.int32),
            pltpu.VMEM((targets, BLK), jnp.int32),
            pltpu.VMEM((1, local), f32),
            pltpu.VMEM((1, local), f32),
            pltpu.VMEM((steps, local), jnp.int32),
            pltpu.VMEM((targets, 2 * edges), jnp.bfloat16),
            pltpu.VMEM((NB, ROWS, BLK), jnp.bfloat16),
            pltpu.VMEM((edges * ROWS, BLK), f32),
            pltpu.VMEM((targets, BLK), jnp.int32),
            pltpu.VMEM((edges, BLK), f32),
            pltpu.VMEM((steps, NB, BLK), f32),
            pltpu.VMEM((DELAYS, targets, BLK), f32),
            pltpu.VMEM((DELAYS, targets, BLK), f32),
            pltpu.VMEM((16, local), f32),
            pltpu.VMEM((steps - 1, areas, NB, BLK), f32),
            pltpu.VMEM((steps - 1, areas, NB, BLK), f32),
            pltpu.VMEM((areas * SHARE, BLK), jnp.bfloat16),
            pltpu.VMEM((areas * SHARE, BLK), jnp.bfloat16),
            pltpu.SemaphoreType.DMA((7,)),
            pltpu.SemaphoreType.DMA((CHUNKS,)),
            pltpu.SemaphoreType.DMA((steps - 1,)),
            pltpu.SemaphoreType.DMA((steps - 1,)),
            pltpu.SemaphoreType.DMA,
            pltpu.SemaphoreType.DMA,
        ],
        compiler_params=pltpu.CompilerParams(
            collective_id=0, has_side_effects=True, vmem_limit_bytes=48 * 1024 * 1024
        ),
    )(
        pattern,
        target_area.reshape(areas, edges),
        target_block.reshape(areas, edges),
        source_block,
        neuron_lag.reshape(targets, BLK),
        tau_mem.reshape(1, local),
        v_init.reshape(1, local),
        ext_count,
    )
    return (volt.reshape(local), act, pend)


def solution(mesh):
    in_specs = (
        P("area", None, None),
        P(),
        P(),
        P(),
        P(),
        P("area"),
        P(("run", "area")),
        P(None, ("run", "area")),
    )
    out_specs = (P(("run", "area")), P(None, ("run", "area")), P(None, ("run", "area")))
    return jax.shard_map(body, mesh=mesh, in_specs=in_specs, out_specs=out_specs, check_vma=False)
```

```python
import functools
import math

import jax
import jax.numpy as jnp
from jax import lax
from jax.experimental import pallas as pl
from jax.experimental.pallas import tpu as pltpu
from jax.sharding import PartitionSpec as P

BLK = 128
NB = 4
DELAYS = 15
ROWS = 16

step_ms = 0.1
ext_gain = 0.25
threshold = 1.0
slope = 4.0
reset_part = 0.5
inhib_gain = 3.0

CHUNKS = 8
SHARE = ROWS * NB


def side_by_side(x):
    return jnp.concatenate([x[b : b + 1, :] for b in range(NB)], axis=1)


def stacked(x):
    return jnp.concatenate([x[:, b * BLK : (b + 1) * BLK] for b in range(NB)], axis=0)


def split(x):
    high = x.astype(jnp.bfloat16)
    low = (x - high.astype(jnp.float32)).astype(jnp.bfloat16)
    return jnp.concatenate([high, low], axis=0)


def kernel(
    areas,
    edges,
    steps,
    pattern,
    route_in,
    tgt_in,
    src_in,
    lag_in,
    tau_in,
    v_in,
    ext_in,
    volt_out,
    act_out,
    pend_out,
    raw,
    weights,
    route,
    tgt,
    src,
    lag,
    tau,
    v_init,
    ext,
    hot,
    inputs,
    terms,
    shift,
    first,
    drive,
    q_lag,
    due,
    acts,
    outbox,
    inbox,
    pend_go,
    pend_in,
    small_sem,
    load_sem,
    send_sem,
    recv_sem,
    fin_send,
    fin_recv,
):
    me = lax.axis_index("area")
    targets = NB * areas
    per = edges // CHUNKS

    small = [
        pltpu.make_async_copy(a, b, small_sem.at[k])
        for k, (a, b) in enumerate(
            [
                (src_in, src),
                (lag_in, lag),
                (route_in, route),
                (tgt_in, tgt),
                (tau_in, tau),
                (v_in, v_init),
                (ext_in, ext),
            ]
        )
    ]
    for copy in small:
        copy.start()

    def load(k):
        return pltpu.make_async_copy(
            pattern.at[pl.ds(k * per, per)], raw.at[pl.ds(k * per, per)], load_sem.at[k]
        )

    for k in range(CHUNKS):
        load(k).start()

    def peer_at(k):
        p = me + k
        return jnp.where(p >= areas, p - areas, p)

    def every_peer(act):
        if areas <= 16:
            for k in sorted(range(1, areas), key=lambda k: -abs(2 * k - areas)):
                act(peer_at(k))
        else:

            def one(k, carry):
                act(peer_at(k))
                return carry

            lax.fori_loop(1, areas, one, 0)

    barrier = pltpu.get_barrier_semaphore()

    def greet(peer):
        pl.semaphore_signal(
            barrier, inc=1, device_id={"area": peer}, device_id_type=pl.DeviceIdType.MESH
        )

    every_peer(greet)
    for copy in small:
        copy.wait()

    where_to = NB * route[pl.ds(me, 1), :] + tgt[pl.ds(me, 1), :]
    ids = lax.broadcasted_iota(jnp.int32, (targets, edges), 0)
    one_hot = (ids == where_to).astype(jnp.float32).astype(jnp.bfloat16)
    hot[:, :edges] = one_hot
    hot[:, edges:] = one_hot
    turned = 2 * lag[...]
    turned = jnp.where(turned >= DELAYS, turned - DELAYS, turned)
    turned = jnp.where(turned >= DELAYS, turned - DELAYS, turned)
    shift[...] = turned
    at_once = jnp.where(turned == 0, 0, DELAYS - turned)
    first[...] = lax.dot_general(
        one_hot,
        at_once.astype(jnp.float32).astype(jnp.bfloat16),
        (((0,), (0,)), ((), ())),
        preferred_element_type=jnp.float32,
    )
    due[...] = jnp.zeros_like(due)
    own_class = []
    for b in range(NB):
        row = lag[pl.ds(me * NB + b, 1), :]
        own_class.append(jnp.where(row >= DELAYS, row - DELAYS, row))
    classes = lax.broadcasted_iota(jnp.int32, (ROWS, BLK), 0)
    alpha = jnp.exp(-step_ms / stacked(tau[...]))
    for t in range(steps):
        drive[t] = ext_gain * (stacked(ext[pl.ds(t, 1), :]).astype(jnp.float32) - 1.5)

    factor = 8.0 / math.sqrt(BLK * edges / NB)
    for k in range(CHUNKS):
        load(k).wait()

        def build(n, carry):
            g = k * (per // 2) + n
            for half in range(2):
                e = 2 * g + half
                sign = jnp.where(src[me * edges + e] == NB - 1, -inhib_gain, 1.0)
                mag = jnp.maximum(raw[e].astype(jnp.float32) - 999.0, 0.0)
                weights[g, pl.ds(half * BLK, BLK), :] = (mag * (sign * (factor / 1000.0))).astype(
                    jnp.bfloat16
                )
            return carry

        lax.fori_loop(0, per // 2, build, 0)

    def think(volt, arrived):
        volt = volt + arrived
        rate = jax.nn.sigmoid(slope * (volt - threshold))
        volt = volt - reset_part * rate
        for b in range(NB):
            inputs[b] = jnp.where(classes == own_class[b], rate[b : b + 1, :], 0.0).astype(
                jnp.bfloat16
            )
        none = jnp.zeros((ROWS, BLK), jnp.bfloat16)

        def multiply(g, carry):
            upper = inputs[src[me * edges + 2 * g]]
            lower = inputs[src[me * edges + 2 * g + 1]]
            both = jnp.concatenate(
                [
                    jnp.concatenate([upper, none], axis=1),
                    jnp.concatenate([none, lower], axis=1),
                ],
                axis=0,
            )
            rows = pl.ds(pl.multiple_of(g * (2 * ROWS), 2 * ROWS), 2 * ROWS)
            terms[rows, :] = jnp.dot(both, weights[g], preferred_element_type=jnp.float32)
            return carry

        lax.fori_loop(0, edges // 2, multiply, 0, unroll=64 if areas <= 16 else 32)
        return volt, rate

    def gather_lags():
        for c in range(DELAYS):
            q_lag[c] = jnp.dot(
                hot[...],
                split(terms[pl.ds(c, edges, stride=ROWS), :]),
                preferred_element_type=jnp.float32,
            )

    def arrivals(rows):
        by = shift[rows, :]
        q = [q_lag[c, rows, :] for c in range(DELAYS)]
        for bit in range(4):
            on = (by & (1 << bit)) != 0
            q = [jnp.where(on, q[(m - (1 << bit)) % DELAYS], q[m]) for m in range(DELAYS)]
        for m in range(DELAYS - 1):
            q[m] = q[m] + due[m + 1, rows, :]
        return q

    def one_step(t, carry):
        volt, arrived = carry
        volt, rate = think(volt, arrived)
        picked = []
        for e in range(0, edges, 32):
            mine = first[pl.ds(e, 32), :]
            y = jnp.zeros((32, BLK), jnp.float32)
            for c in range(DELAYS):
                y = jnp.where(mine == float(c), terms[pl.ds(e * ROWS + c, 32, stride=ROWS), :], y)
            picked.append(y)
        soon = due[1] + jnp.dot(
            hot[...], split(jnp.concatenate(picked, axis=0)), preferred_element_type=jnp.float32
        )
        for a in range(areas):
            outbox[t, a] = soon[a * NB : (a + 1) * NB, :]

        def send(peer):
            pltpu.make_async_remote_copy(
                src_ref=outbox.at[t, peer],
                dst_ref=inbox.at[t, me],
                send_sem=send_sem.at[t],
                recv_sem=recv_sem.at[t],
                device_id={"area": peer},
                device_id_type=pl.DeviceIdType.MESH,
            ).start()

        every_peer(send)
        inbox[t, me] = outbox[t, me]
        acts[pl.ds(t, 1), :] = side_by_side(rate)
        gather_lags()

        def turn(r, carry):
            rows = pl.ds(pl.multiple_of(r * 8, 8), 8)
            q = arrivals(rows)
            for m in range(DELAYS):
                due[m, rows, :] = q[m]
            return carry

        lax.fori_loop(0, targets // 8, turn, 0)
        ahead = alpha * volt + drive[t + 1]
        step_messages(t).wait_recv()
        return ahead, jnp.sum(inbox[t], axis=0)

    def step_messages(t):
        return pltpu.make_async_remote_copy(
            src_ref=outbox.at[t, pl.ds(0, areas - 1)],
            dst_ref=inbox.at[t, pl.ds(0, areas - 1)],
            send_sem=send_sem.at[t],
            recv_sem=recv_sem.at[t],
            device_id={"area": me},
            device_id_type=pl.DeviceIdType.MESH,
        )

    pl.semaphore_wait(barrier, areas - 1)
    volt, arrived = lax.fori_loop(
        0, steps - 1, one_step, (alpha * stacked(v_init[...]) + drive[0], jnp.zeros((NB, BLK), jnp.float32))
    )
    volt, rate = think(volt, arrived)
    gather_lags()

    def share(a):
        return pl.ds(pl.multiple_of(a * SHARE, SHARE), SHARE)

    def last(n, carry):
        r = n + me // 2 + 1
        r = jnp.where(r >= areas // 2, r - areas // 2, r)
        q = arrivals(pl.ds(pl.multiple_of(r * 8, 8), 8))
        for half in range(2):
            peer = 2 * r + half
            parts = [q[m][half * NB : (half + 1) * NB, :] for m in range(DELAYS)]
            parts.append(jnp.zeros((NB, BLK), jnp.float32))
            pend_go[share(peer), :] = jnp.concatenate(parts, axis=0).astype(jnp.bfloat16)

            @pl.when(peer != me)
            def _():
                pltpu.make_async_remote_copy(
                    src_ref=pend_go.at[share(peer)],
                    dst_ref=pend_in.at[share(me)],
                    send_sem=fin_send,
                    recv_sem=fin_recv,
                    device_id={"area": peer},
                    device_id_type=pl.DeviceIdType.MESH,
                ).start()

        return carry

    lax.fori_loop(0, areas // 2, last, 0, unroll=4)
    acts[pl.ds(steps - 1, 1), :] = side_by_side(rate)
    pend_in[share(me), :] = pend_go[share(me), :]
    volt_out[...] = side_by_side(volt)
    act_out[...] = acts[pl.ds(0, steps), :].astype(jnp.bfloat16)
    for t in range(steps - 1):
        step_messages(t).wait_send()
    everything = pltpu.make_async_remote_copy(
        src_ref=pend_go.at[pl.ds(0, (areas - 1) * SHARE)],
        dst_ref=pend_in.at[pl.ds(0, (areas - 1) * SHARE)],
        send_sem=fin_send,
        recv_sem=fin_recv,
        device_id={"area": me},
        device_id_type=pl.DeviceIdType.MESH,
    )
    everything.wait_recv()
    total = jnp.zeros((SHARE, BLK), jnp.float32)
    for a in range(areas):
        total = total + pend_in[pl.ds(a * SHARE, SHARE), :].astype(jnp.float32)
    for m in range(DELAYS):
        pend_out[pl.ds(m, 1), :] = side_by_side(total[m * NB : (m + 1) * NB, :])
    everything.wait_send()


def body(pattern, target_area, source_block, target_block, neuron_lag, tau_mem, v_init, ext_count):
    areas = lax.axis_size("area")
    edges = pattern.shape[0]
    steps, local = ext_count.shape
    vmem = pl.BlockSpec(memory_space=pltpu.VMEM)
    hbm = pl.BlockSpec(memory_space=pltpu.HBM)
    targets = areas * NB
    f32 = jnp.float32
    volt, act, pend = pl.pallas_call(
        functools.partial(kernel, areas, edges, steps),
        out_shape=(
            jax.ShapeDtypeStruct((1, local), f32),
            jax.ShapeDtypeStruct((steps, local), jnp.bfloat16),
            jax.ShapeDtypeStruct((DELAYS, local), f32),
        ),
        in_specs=[hbm] * 8,
        out_specs=(vmem, vmem, vmem),
        scratch_shapes=[
            pltpu.VMEM((edges, BLK, BLK), jnp.int32),
            pltpu.VMEM((edges // 2, 2 * BLK, BLK), jnp.bfloat16),
            pltpu.VMEM((areas, edges), jnp.int32),
            pltpu.VMEM((areas, edges), jnp.int32),
            pltpu.SMEM((areas * edges,), jnp.int32),
            pltpu.VMEM((targets, BLK), jnp.int32),
            pltpu.VMEM((1, local), f32),
            pltpu.VMEM((1, local), f32),
            pltpu.VMEM((steps, local), jnp.int32),
            pltpu.VMEM((targets, 2 * edges), jnp.bfloat16),
            pltpu.VMEM((NB, ROWS, BLK), jnp.bfloat16),
            pltpu.VMEM((edges * ROWS, BLK), f32),
            pltpu.VMEM((targets, BLK), jnp.int32),
            pltpu.VMEM((edges, BLK), f32),
            pltpu.VMEM((steps, NB, BLK), f32),
            pltpu.VMEM((DELAYS, targets, BLK), f32),
            pltpu.VMEM((DELAYS, targets, BLK), f32),
            pltpu.VMEM((16, local), f32),
            pltpu.VMEM((steps - 1, areas, NB, BLK), f32),
            pltpu.VMEM((steps - 1, areas, NB, BLK), f32),
            pltpu.VMEM((areas * SHARE, BLK), jnp.bfloat16),
            pltpu.VMEM((areas * SHARE, BLK), jnp.bfloat16),
            pltpu.SemaphoreType.DMA((7,)),
            pltpu.SemaphoreType.DMA((CHUNKS,)),
            pltpu.SemaphoreType.DMA((steps - 1,)),
            pltpu.SemaphoreType.DMA((steps - 1,)),
            pltpu.SemaphoreType.DMA,
            pltpu.SemaphoreType.DMA,
        ],
        compiler_params=pltpu.CompilerParams(
            collective_id=0, has_side_effects=True, vmem_limit_bytes=48 * 1024 * 1024
        ),
    )(
        pattern,
        target_area.reshape(areas, edges),
        target_block.reshape(areas, edges),
        source_block,
        neuron_lag.reshape(targets, BLK),
        tau_mem.reshape(1, local),
        v_init.reshape(1, local),
        ext_count,
    )
    return (volt.reshape(local), act, pend)


def solution(mesh):
    in_specs = (
        P("area", None, None),
        P(),
        P(),
        P(),
        P(),
        P("area"),
        P(("run", "area")),
        P(None, ("run", "area")),
    )
    out_specs = (P(("run", "area")), P(None, ("run", "area")), P(None, ("run", "area")))
    return jax.shard_map(body, mesh=mesh, in_specs=in_specs, out_specs=out_specs, check_vma=False)
```
